256 devices in a mesh: pipe: 16 (over y_hi, z), dp: 16 (over x, y_lo, core).
Axes of the slice: x: 4, y: 4 (y_hi: 2, y_lo: 2; y = y_hi * 2 + y_lo), z: 8, core: 2. Of those that a mesh axis runs over, the one named last changes fastest.
Arguments:
- stash: bfloat16 [16, 2048, 12288], P('pipe', 'dp'), may hold values from -6 to 6
- grad_in: bfloat16 [16, 2048, 12288], P('pipe', 'dp'), may hold values from -6 to 6
- base_back: bfloat16 [16, 2048, 12288], P('pipe', 'dp'), may hold values from -6 to 6
- gain: bfloat16 [16, 12288], P('pipe'), may hold values from 0.5 to 1.5
- w_down: bfloat16 [16, 64, 12288], P('pipe', None, 'dp'), may hold values from -0.75 to 0.75
- w_up: bfloat16 [16, 64, 12288], P('pipe', None, 'dp'), may hold values from -0.0546875 to 0.0546875
- mom_down: bfloat16 [16, 64, 12288], P('pipe', None, 'dp'), may hold values from -0.046875 to 0.046875
- mom_up: bfloat16 [16, 64, 12288], P('pipe', None, 'dp'), may hold values from -0.4375 to 0.4375
Outputs:
- grad_prev: bfloat16 [16, 2048, 12288], P('pipe', 'dp')
- step_first: bfloat16 [16, 64, 12288], P('pipe', None, 'dp')
- step_second: bfloat16 [16, 64, 12288], P('pipe', None, 'dp')
- moment_first: bfloat16 [16, 64, 12288], P('pipe', None, 'dp')
- moment_second: bfloat16 [16, 64, 12288], P('pipe', None, 'dp')
The draws below stay inside these ranges and needn't reach their ends.
All inputs are finite; a program needn't handle non-finite values.
Results may differ from the reference program's by a relative error of at most 0.039.
Values may be sent and summed in bfloat16 or wider, within the bound.
A program may use at most 64 MiB of HBM per device.

```python
import jax
import jax.numpy as jnp
from jax import lax

D = 12288
RANK = 64
ROWS = 128
TOKENS = 2048
N_PIPE = 16
N_DP = 16


def stash_field(key, scale_low, scale_high):
    key = jax.random.fold_in(key, 101)
    noise_key, scale_key, pair_key = jax.random.split(key, 3)
    raw = jax.random.normal(noise_key, (N_PIPE, TOKENS, D), jnp.float32)
    row_scale = jax.random.uniform(scale_key, (N_PIPE, TOKENS, 1), jnp.float32, scale_low, scale_high)
    pairing = jax.vmap(lambda section_key: jax.random.permutation(section_key, N_DP))(jax.random.split(pair_key, N_PIPE))
    token_block = jnp.arange(TOKENS) // ROWS
    feature_block = jnp.arange(D) // (D // N_DP)
    target = pairing[:, token_block]
    paired = (target[:, :, None] == feature_block[None, None, :]).astype(jnp.float32)
    field = raw * row_scale * (1.0 + 2.0 * paired)
    return jnp.clip(field, -6.0, 6.0)


def draw_stash(key, part):
    field = stash_field(key, 1.0, 1.0)
    return field.astype(jnp.bfloat16)


def draw_base_back(key, part):
    field = stash_field(key, 1.0, 1.0)
    key = jax.random.fold_in(key, 5)
    noise = jax.random.normal(key, (N_PIPE, TOKENS, D), jnp.float32)
    layer_inputs = jnp.roll(field, -(N_PIPE // 2), axis=0)
    mixed = 0.7 * layer_inputs + 0.7 * noise
    return jnp.clip(mixed, -6.0, 6.0).astype(jnp.bfloat16)


def with_spikes(result, key, source, target, parts, factor):
    owner, partner = [(jnp.arange(result.shape[position]) // (result.shape[position] // parts)).reshape([-1 if axis == position else 1 for axis in range(result.ndim)]) for position in (source, target)]
    chosen = jax.random.permutation(key, parts)[partner]
    strong = (owner == chosen) | (owner == (partner + parts // 2) % parts)
    return jnp.where(strong, factor * result, result)


def levels(own_key, extent, cuts, least, top_value):
    factor_of = 1.0
    for dim, blocks in cuts:
        steps = jax.random.uniform(jax.random.fold_in(jax.random.fold_in(own_key, 6), dim), (blocks,), jnp.float32, least / len(cuts), top_value / len(cuts))
        factor_of = factor_of * jnp.repeat(jnp.exp(steps), extent[dim] // blocks).reshape((-1,) + (1,) * (len(extent) - 1 - dim))
    return factor_of


def scatter_about(stream_key, shape, spread, most, pieces=(), kind=jnp.bfloat16):
    result = spread * jax.random.normal(stream_key, shape, jnp.float32)
    if pieces:
        result = result * levels(stream_key, shape, pieces, -0.22, 0.18)
    return jnp.clip(result, -most, most).astype(kind)


def bell_draw_with(own_key, dims, spread, bound, shards, heavy, kind=jnp.bfloat16):
    values = spread * jax.random.normal(own_key, dims, jnp.float32)
    if shards:
        values = values * levels(own_key, dims, shards, -0.22, 0.18)
    return jnp.clip(with_spikes(values, jax.random.fold_in(own_key, 3), *heavy), -bound, bound).astype(kind)


def setup_inputs(seed: int = 0) -> dict:
    streams_of = jax.random.split(jax.random.key(seed), 9)
    return {
        "stash": draw_stash(jax.random.fold_in(streams_of[8], 71), 0),
        "grad_in": bell_draw_with(streams_of[1], (N_PIPE, TOKENS, D), 1.0, 6.0, ((0, 16), (1, 16)), (1, 2, 16, 2.0)),
        "base_back": draw_base_back(jax.random.fold_in(streams_of[8], 71), 0),
        "gain": jnp.clip(1.0 + 0.1 * jax.random.normal(streams_of[3], (N_PIPE, D), jnp.float32), 0.5, 1.5).astype(jnp.bfloat16),
        "w_down": scatter_about(streams_of[4], (N_PIPE, RANK, D), RANK ** -0.5, 0.75, ((0, 16), (2, 16))),
        "w_up": scatter_about(streams_of[5], (N_PIPE, RANK, D), D ** -0.5, 0.0546875, ((0, 16), (2, 16))),
        "mom_down": scatter_about(streams_of[6], (N_PIPE, RANK, D), 0.003, 0.046875, ((0, 16), (2, 16))),
        "mom_up": scatter_about(streams_of[7], (N_PIPE, RANK, D), 0.03, 0.4375, ((0, 16), (2, 16))),
    }


norm_eps = 1e-05
beta_one = 0.9
beta_two = 0.99
lion_delta = 0.003

def normalize(saved_rows, gain_row):
    values = saved_rows.astype(jnp.float32)
    average = lax.optimization_barrier(jnp.mean(values, axis=-1, keepdims=True))
    centred = values - average
    variance = lax.optimization_barrier(jnp.mean(centred * centred, axis=-1, keepdims=True))
    inverse = lax.rsqrt(variance + norm_eps)
    unit_rows = centred * inverse
    normed = (unit_rows * gain_row).astype(jnp.bfloat16)
    return (unit_rows, inverse, normed)

def norm_backward(back_norm, gain_row, unit_rows, inverse):
    scaled = back_norm * gain_row
    first_mean = lax.optimization_barrier(jnp.mean(scaled, axis=-1, keepdims=True))
    second_mean = lax.optimization_barrier(jnp.mean(scaled * unit_rows, axis=-1, keepdims=True))
    return (inverse * (scaled - first_mean - unit_rows * second_mean)).astype(jnp.bfloat16)

def lion(moment, gradient):
    blend = beta_one * moment + (1.0 - beta_one) * gradient
    direction = (blend / (jnp.abs(blend) + lion_delta)).astype(jnp.bfloat16)
    renewed = (beta_two * moment + (1.0 - beta_two) * gradient).astype(jnp.bfloat16)
    return (direction, renewed)

def reference(stash, grad_in, base_back, gain, w_down, w_up, mom_down, mom_up):
    saved_all = jnp.roll(stash, -(N_PIPE // 2), axis=0)

    def section(section_items):
        saved_rows, grad_rows, base_rows, gain_vec, down_map, up_map, moment_first, moment_second = section_items
        gain_row = gain_vec.astype(jnp.float32)

        def one_group(running, block_items):
            group_saved, group_grad, group_base = block_items
            unit_rows, inverse, normed = normalize(group_saved, gain_row)
            low_rows = jnp.dot(normed, down_map.T, preferred_element_type=jnp.float32).astype(jnp.bfloat16)
            delta_rows = jnp.dot(group_grad, up_map.T, preferred_element_type=jnp.float32).astype(jnp.bfloat16)
            back_norm = group_base.astype(jnp.float32) + jnp.dot(delta_rows, down_map, preferred_element_type=jnp.float32)
            grad_input = norm_backward(back_norm, gain_row, unit_rows, inverse)
            part_first = lax.optimization_barrier((jnp.dot(delta_rows.T, normed, preferred_element_type=jnp.float32) / TOKENS).astype(jnp.bfloat16)).astype(jnp.float32)
            part_second = lax.optimization_barrier((jnp.dot(low_rows.T, group_grad, preferred_element_type=jnp.float32) / TOKENS).astype(jnp.bfloat16)).astype(jnp.float32)
            return ((running[0] + part_first, running[1] + part_second), grad_input)
        start_sums = (jnp.zeros((RANK, D), jnp.float32), jnp.zeros((RANK, D), jnp.float32))
        (grad_first, grad_second), grad_inputs = lax.scan(one_group, start_sums, (saved_rows.reshape(N_DP, ROWS, D), grad_rows.reshape(N_DP, ROWS, D), base_rows.reshape(N_DP, ROWS, D)))
        step_first, new_first = lion(moment_first.astype(jnp.float32), grad_first)
        step_second, new_second = lion(moment_second.astype(jnp.float32), grad_second)
        return (grad_inputs.reshape(TOKENS, D), step_first, step_second, new_first, new_second)
    grad_inputs, step_first, step_second, moment_first, moment_second = lax.map(section, (saved_all, grad_in, base_back, gain, w_down, w_up, mom_down, mom_up))
    grad_prev = jnp.concatenate([grad_inputs[1:], jnp.zeros_like(grad_inputs[:1])], axis=0)
    return (grad_prev, step_first, step_second, moment_first, moment_second)
```

```python
import functools

import jax
import jax.numpy as jnp
from jax import lax
from jax.experimental import pallas as pl
from jax.experimental.pallas import tpu as pltpu
from jax.sharding import PartitionSpec as P

norm_eps = 1e-05
beta_one = 0.9
beta_two = 0.99
lion_delta = 0.003

D = 12288
RANK = 64
ROWS = 128
TOKENS = 2048
SHARE = D // 16
CHUNK = 16
CHUNKS = ROWS // CHUNK
WIDE = 1536
WIDES = D // WIDE
MESH = pl.DeviceIdType.MESH
f32 = jnp.float32
bf16 = jnp.bfloat16

contract_last = (((1,), (1,)), ((), ()))


def dot_last(a, b):
    return lax.dot_general(a, b, contract_last, preferred_element_type=f32)


def fold(v):
    parts = [v[:, i : i + 128] for i in range(0, v.shape[1], 128)]
    while len(parts) > 1:
        half = [a + b for a, b in zip(parts[::2], parts[1::2])]
        if len(parts) % 2:
            half.append(parts[-1])
        parts = half
    return parts[0]


def row_sum(acc):
    return jnp.sum(acc, axis=1, keepdims=True)


def main_kernel(
    stash, grad, base, gain, w_down, w_up,
    gp, g1_out, g2_out,
    st, sv, gr, ba, b, W, WS, gain_own, gain_far,
    delta_own, delta_far, low_own, low_far, b_mean, inv_row,
    part_send, part_keep, part_recv, sum_send, sum_recv,
    cross_send, cross_recv, pair_send, pair_recv, kept,
    local_sem, send_sem, recv_sem,
):
    s = lax.axis_index("pipe")
    d = lax.axis_index("dp")
    x, yl, c = d // 4, (d // 2) % 2, d % 2
    far = (s + 8) % 16
    z = s % 8
    z_down = s - z + (z + 7) % 8
    z_up = s - z + (z + 1) % 8
    d_pair = d + 2 - 4 * yl
    d_core = d + 1 - 2 * c
    d_x = [(d + 4 * o) % 16 for o in (1, 2, 3)]
    own = x * 4 + c * 2 + yl
    pair = x * 4 + c * 2 + 1 - yl
    first = x * 4 + c * 2

    def remote(src, dst, sem, device):
        return pltpu.make_async_remote_copy(
            src_ref=src, dst_ref=dst, send_sem=send_sem.at[sem], recv_sem=recv_sem.at[sem],
            device_id=device, device_id_type=MESH,
        )

    def feature(e):
        return (e // 4) * 4 + (e % 2) * 2 + (e // 2) % 2

    def columns(f):
        return pl.ds(pl.multiple_of(f * SHARE, 128), SHARE)

    def wide(i):
        return pl.ds(pl.multiple_of(i * WIDE, 128), WIDE)

    def chunk_rows(k):
        if isinstance(k, int):
            return pl.ds(k * CHUNK, CHUNK)
        return pl.ds(pl.multiple_of(k * CHUNK, CHUNK), CHUNK)

    loads = [
        pltpu.make_async_copy(w_down.at[0], W.at[own, 0], local_sem.at[0]),
        pltpu.make_async_copy(w_up.at[0], W.at[own, 1], local_sem.at[1]),
        pltpu.make_async_copy(stash, st, local_sem.at[2]),
        pltpu.make_async_copy(grad, gr, local_sem.at[3]),
        pltpu.make_async_copy(base, ba, local_sem.at[4]),
    ]
    for load in loads:
        load.start()
    gain_own[...] = gain[...].astype(f32)

    barrier = pltpu.get_barrier_semaphore()
    partners = [(far, d), (z_down, d), (z_up, d), (s, d_pair), (s, d_core), (far, d_pair)]
    partners += [(s, t) for t in d_x]
    for t in partners:
        pl.semaphore_signal(barrier, inc=1, device_id=t, device_id_type=MESH)
    pl.semaphore_wait(barrier, len(partners))

    w_pair = remote(W.at[own], W.at[own], 0, (s, d_pair))
    w_x_own = [remote(W.at[own], W.at[own], 1 + i, (s, t)) for i, t in enumerate(d_x)]
    w_x_pair = [remote(W.at[pair], W.at[pair], 4 + i, (s, t)) for i, t in enumerate(d_x)]

    def group(buf, xs):
        return buf.at[pl.ds(xs * 4 + c * 2, 2)]

    def group_down(xs):
        return W.at[pl.ds(xs * 4 + c * 2, 2), 0]

    x_from = [(x + 4 - o) % 4 for o in range(4)]
    w_core = [remote(group(W, x_from[o]), group(W, x_from[o]), 7 + o, (s, d_core)) for o in range(4)]
    ws_far = remote(group_down(x), group(WS, x), 11, (far, d_pair))
    ws_x = [remote(group(WS, x), group(WS, x), 12 + i, (s, t)) for i, t in enumerate(d_x)]
    ws_core = [remote(group(WS, x_from[o]), group(WS, x_from[o]), 15 + o, (s, d_core)) for o in range(4)]
    gain_copy = remote(gain_own, gain_far, 19, (far, d))
    delta_copy = remote(delta_own, delta_far, 20, (far, d))
    low_copy = remote(low_own, low_far, 21, (far, d))
    part_copy = remote(part_send, part_recv, 22, (s, d_core))
    sum_copy = [remote(sum_send.at[(x + o) % 4], sum_recv.at[o - 1], 22 + o, (s, d_x[o - 1])) for o in (1, 2, 3)]
    cross_copy = remote(cross_send, cross_recv, 26, (far, d_pair))
    pair_copy = remote(pair_send, pair_recv, 27, (s, d_pair))

    def stash_copy(k):
        return remote(stash.at[chunk_rows(k)], sv.at[chunk_rows(k)], 28 + k, (far, d))

    def relay_copy(k):
        return remote(sv.at[chunk_rows(k)], sv.at[chunk_rows(k)], 28 + k, (far, d))

    def z_copy(k):
        return remote(sv.at[chunk_rows(k)], gp.at[chunk_rows(k)], 28 + CHUNKS + k, (z_down, d))

    loads[0].wait()
    loads[1].wait()
    w_pair.start()
    for copy in w_x_own:
        copy.start()
    gain_copy.start()

    @pl.when(s != 8)
    def _():
        for k in range(CHUNKS):
            stash_copy(k).start()

    loads[2].wait()

    def mean_and_inverse(ref, rows, extra=None):
        def add(i, acc):
            return acc + fold(ref[rows, wide(i)].astype(f32))

        zero = jnp.zeros((CHUNK, 128), f32)
        mean = row_sum(lax.fori_loop(0, WIDES, add, zero)) * (1.0 / D)

        def add_square(i, acc):
            centred = ref[rows, wide(i)].astype(f32) - mean
            total = acc[0] + fold(centred * centred)
            if extra is None:
                return (total,)
            return (total, acc[1] + fold(centred * extra[rows, wide(i)]))

        sums = lax.fori_loop(0, WIDES, add_square, (zero,) if extra is None else (zero, zero))
        inverse = lax.rsqrt(row_sum(sums[0]) * (1.0 / D) + norm_eps)
        if extra is None:
            return mean, inverse
        return mean, inverse, row_sum(sums[1]) * (1.0 / D)

    def row_stats(r, carry):
        rows = chunk_rows(r)
        mean, inverse = mean_and_inverse(st, rows)
        b_mean[rows, :] = mean
        inv_row[rows, :] = inverse
        return carry

    lax.fori_loop(0, CHUNKS, row_stats, 0)

    w_pair.wait_recv()
    for copy in w_x_pair:
        copy.start()
    ws_far.start()
    w_core[0].start()

    gain_copy.wait_recv()

    def write_normed(r, carry):
        rows = chunk_rows(r)
        mean, inverse = b_mean[rows, :], inv_row[rows, :]

        def one(i, carry):
            centred = st[rows, wide(i)].astype(f32) - mean
            st[rows, wide(i)] = ((centred * inverse) * gain_far[:, wide(i)]).astype(bf16)
            return carry

        return lax.fori_loop(0, WIDES, one, carry)

    lax.fori_loop(0, CHUNKS, write_normed, 0)

    ws_far.wait_recv()
    for copy in ws_x:
        copy.start()
    ws_core[0].start()

    for o in (1, 3, 2):
        w_x_own[o - 1].wait_recv()
        w_x_pair[o - 1].wait_recv()
        w_core[o].start()
    loads[3].wait()
    loads[4].wait()
    for o in (0, 1, 3, 2):
        w_core[o].wait_recv()

    def add_delta(e, acc):
        return acc + dot_last(gr[:, columns(feature(e))], W[e, 1])

    delta = lax.fori_loop(0, 16, add_delta, jnp.zeros((ROWS, RANK), f32))
    delta_own[...] = jnp.zeros((ROWS, 128), bf16)
    delta_own[:, :RANK] = delta.astype(bf16)
    delta_copy.start()

    def write_b(e, acc):
        cols = columns(feature(e))
        back = jnp.dot(delta_own[:, :RANK], W[e, 0], preferred_element_type=f32)
        value = (ba[:, cols].astype(f32) + back) * gain_own[:, cols]
        b[:, cols] = value
        return acc + fold(value)

    b_sum = lax.fori_loop(0, 16, write_b, jnp.zeros((ROWS, 128), f32))
    b_mean[...] = row_sum(b_sum) * (1.0 / D)

    def grad_chunk(k):
        rows = chunk_rows(k)
        mean, inverse, cross = mean_and_inverse(sv, rows, b)
        first_mean = b_mean[rows, :]
        second_mean = cross * inverse

        def one(i, carry):
            unit = (sv[rows, wide(i)].astype(f32) - mean) * inverse
            value = inverse * (b[rows, wide(i)] - first_mean - unit * second_mean)
            sv[rows, wide(i)] = value.astype(bf16)
            return carry

        lax.fori_loop(0, WIDES, one, 0)

    def step(k):
        @pl.when(s != 0)
        def _():
            stash_copy(k).wait_recv()
            grad_chunk(k)

        @pl.when(s == 8)
        def _():
            relay_copy(k).start()

        @pl.when(jnp.logical_and(s != 0, s != 8))
        def _():
            z_copy(k).start()

        if k > 0:
            relay(k - 1)

    def relay(k):
        @pl.when(s == 0)
        def _():
            relay_copy(k).wait_recv()
            z_copy(k).start()

    step(0)
    step(1)

    for o in (1, 3, 2):
        ws_x[o - 1].wait_recv()
        ws_core[o].start()

    step(2)

    for o in (0, 1, 3, 2):
        ws_core[o].wait_recv()

    def add_low(e, acc):
        return acc + dot_last(st[:, columns(feature(e))], WS[e])

    low = lax.fori_loop(0, 16, add_low, jnp.zeros((ROWS, RANK), f32))
    low_own[...] = jnp.zeros((ROWS, 128), bf16)
    low_own[:, :RANK] = low.astype(bf16)
    low_copy.start()

    step(3)

    delta_copy.wait_recv()
    low_copy.wait_recv()
    delta_t = delta_far[...].astype(f32).T[:RANK].astype(bf16)
    low_t = low_far[...].astype(f32).T[:RANK].astype(bf16)

    def write_parts(j, carry):
        f = (j // 2) * 4 + (j % 2) * 2
        for buf, core in ((part_keep, c), (part_send, 1 - c)):
            cols = columns(f + core)
            one = jnp.dot(delta_t, st[:, cols], preferred_element_type=f32) * (1.0 / TOKENS)
            two = jnp.dot(low_t, gr[:, cols], preferred_element_type=f32) * (1.0 / TOKENS)
            buf[j, 0] = one.astype(bf16)
            buf[j, 1] = two.astype(bf16)
        return carry

    lax.fori_loop(0, 8, write_parts, 0)
    part_copy.start()

    step(4)

    part_copy.wait_recv()

    def add_parts(j, carry):
        total = part_keep[j].astype(f32) + part_recv[j].astype(f32)
        sum_send[j // 2, j % 2] = total.astype(bf16)
        return carry

    lax.fori_loop(0, 8, add_parts, 0)
    for copy in sum_copy:
        copy.start()

    step(5)

    for copy in sum_copy:
        copy.wait_recv()

    def total_of(y, kind):
        total = sum_send[x, y, kind].astype(f32)
        for i in range(3):
            total = total + sum_recv[i, y, kind].astype(f32)
        return total

    for y in range(2):
        cross_send[y] = total_of(y, 0).astype(bf16)
    cross_copy.start()
    pair_send[1] = total_of(1 - yl, 1).astype(bf16)
    kept[...] = total_of(yl, 1)

    step(6)

    cross_copy.wait_recv()
    pair_send[0] = cross_recv[1 - yl]
    pair_copy.start()

    step(7)

    pair_copy.wait_recv()
    g1_out[...] = cross_recv[yl].astype(f32) + pair_recv[0].astype(f32)
    g2_out[...] = kept[...] + pair_recv[1].astype(f32)

    @pl.when(s == 15)
    def _():
        ba[...] = jnp.zeros_like(ba)
        zeros = pltpu.make_async_copy(ba, gp, local_sem.at[5])
        zeros.start()
        zeros.wait()

    relay(CHUNKS - 1)

    sent = [w_pair, *w_x_own, *w_x_pair, *w_core, ws_far, *ws_x, *ws_core]
    sent += [gain_copy, delta_copy, low_copy, part_copy, *sum_copy, cross_copy, pair_copy]
    for copy in sent:
        copy.wait_send()
    for k in range(CHUNKS):
        stash_copy(k).wait_send()

        @pl.when(s != 8)
        def _():
            z_copy(k).wait_send()

        @pl.when(s != 15)
        def _():
            z_copy(k).wait_recv()


def lion(moment, gradient):
    blend = beta_one * moment + (1.0 - beta_one) * gradient
    direction = (blend / (jnp.abs(blend) + lion_delta)).astype(bf16)
    renewed = (beta_two * moment + (1.0 - beta_two) * gradient).astype(bf16)
    return direction, renewed


def shards(stash, grad_in, base_back, gain, w_down, w_up, mom_down, mom_up):
    hbm = pl.BlockSpec(memory_space=pl.ANY)
    vmem = pl.BlockSpec(memory_space=pltpu.VMEM)
    share = (RANK, SHARE)
    upstream, grad_first, grad_second = pl.pallas_call(
        main_kernel,
        out_shape=(
            jax.ShapeDtypeStruct((ROWS, D), bf16),
            jax.ShapeDtypeStruct(share, f32),
            jax.ShapeDtypeStruct(share, f32),
        ),
        in_specs=[hbm, hbm, hbm, vmem, hbm, hbm],
        out_specs=(hbm, vmem, vmem),
        scratch_shapes=[
            pltpu.VMEM((ROWS, D), bf16),
            pltpu.VMEM((ROWS, D), bf16),
            pltpu.VMEM((ROWS, D), bf16),
            pltpu.VMEM((ROWS, D), bf16),
            pltpu.VMEM((ROWS, D), f32),
            pltpu.VMEM((16, 2) + share, bf16),
            pltpu.VMEM((16,) + share, bf16),
            pltpu.VMEM((1, D), f32),
            pltpu.VMEM((1, D), f32),
            pltpu.VMEM((ROWS, 128), bf16),
            pltpu.VMEM((ROWS, 128), bf16),
            pltpu.VMEM((ROWS, 128), bf16),
            pltpu.VMEM((ROWS, 128), bf16),
            pltpu.VMEM((ROWS, 1), f32),
            pltpu.VMEM((ROWS, 1), f32),
            pltpu.VMEM((8, 2) + share, bf16),
            pltpu.VMEM((8, 2) + share, bf16),
            pltpu.VMEM((8, 2) + share, bf16),
            pltpu.VMEM((4, 2, 2) + share, bf16),
            pltpu.VMEM((3, 2, 2) + share, bf16),
            pltpu.VMEM((2,) + share, bf16),
            pltpu.VMEM((2,) + share, bf16),
            pltpu.VMEM((2,) + share, bf16),
            pltpu.VMEM((2,) + share, bf16),
            pltpu.VMEM(share, f32),
            pltpu.SemaphoreType.DMA((6,)),
            pltpu.SemaphoreType.DMA((28 + 2 * CHUNKS,)),
            pltpu.SemaphoreType.DMA((28 + 2 * CHUNKS,)),
        ],
        compiler_params=pltpu.CompilerParams(
            collective_id=0, has_side_effects=True, vmem_limit_bytes=52 * 1024 * 1024
        ),
        cost_estimate=pl.CostEstimate(flops=2 * 5 * ROWS * D * RANK, bytes_accessed=16 * ROWS * D, transcendentals=0),
        name="block",
    )(stash[0], grad_in[0], base_back[0], gain, w_down, w_up)
    step_first, moment_first = lion(mom_down[0].astype(f32), grad_first)
    step_second, moment_second = lion(mom_up[0].astype(f32), grad_second)
    return (
        upstream[None],
        step_first[None],
        step_second[None],
        moment_first[None],
        moment_second[None],
    )


def solution(mesh):
    rows = P("pipe", "dp", None)
    share = P("pipe", None, "dp")
    return jax.shard_map(
        shards,
        mesh=mesh,
        in_specs=(rows, rows, rows, P("pipe", None), share, share, share, share),
        out_specs=(rows, share, share, share, share),
        check_vma=False,
    )
```

```python
import functools

import jax
import jax.numpy as jnp
from jax import lax
from jax.experimental import pallas as pl
from jax.experimental.pallas import tpu as pltpu
from jax.sharding import PartitionSpec as P

norm_eps = 1e-05
beta_one = 0.9
beta_two = 0.99
lion_delta = 0.003

D = 12288
RANK = 64
ROWS = 128
TOKENS = 2048
SHARE = D // 16
CHUNK = 16
CHUNKS = ROWS // CHUNK
WIDE = 1536
WIDES = D // WIDE
PARTS = 4
PART = D // PARTS
CORE = 48 + CHUNKS * PARTS
SEMS = CORE + 8
MESH = pl.DeviceIdType.MESH
VMEM_LIMIT = 63 * 1024 * 1024
f32 = jnp.float32
bf16 = jnp.bfloat16

contract_last = (((1,), (1,)), ((), ()))


def dot_last(a, b):
    return lax.dot_general(a, b, contract_last, preferred_element_type=f32)


def fold(v):
    parts = [v[:, i : i + 128] for i in range(0, v.shape[1], 128)]
    while len(parts) > 1:
        half = [a + b for a, b in zip(parts[::2], parts[1::2])]
        if len(parts) % 2:
            half.append(parts[-1])
        parts = half
    return parts[0]


def row_sum(acc):
    return jnp.sum(acc, axis=1, keepdims=True)


def lion(moment, gradient):
    blend = beta_one * moment + (1.0 - beta_one) * gradient
    direction = (blend / (jnp.abs(blend) + lion_delta)).astype(bf16)
    renewed = (beta_two * moment + (1.0 - beta_two) * gradient).astype(bf16)
    return direction, renewed


def main_kernel(
    stash, grad, base, gain, w_down, w_up, mom_down, mom_up,
    gp, step1, step2, new1, new2,
    m1, m2,    gain_in, gain_land, st, sv, gr, ba, b, W, WS, gain_own, gain_far,
    delta_own, delta_far, low_own, low_far, b_mean, mean_row, inv_row,
    part_send, part_keep, part_recv, sum_send, sum_recv,
    pair_send, pair_recv, kept, final_send, final_recv,
    local_sem, send_sem, recv_sem,
):
    s = lax.axis_index("pipe")
    d = lax.axis_index("dp")
    x, yl, c = d // 4, (d // 2) % 2, d % 2
    far = (s + 8) % 16
    z = s % 8
    z_down = s - z + (z + 7) % 8
    z_up = s - z + (z + 1) % 8
    d_pair = d + 2 - 4 * yl
    d_core = d + 1 - 2 * c
    d_x = [(d + 4 * o) % 16 for o in (1, 2, 3)]
    own = x * 4 + c * 2 + yl
    pair = x * 4 + c * 2 + 1 - yl
    first = x * 4 + c * 2

    def remote(src, dst, sem, device):
        return pltpu.make_async_remote_copy(
            src_ref=src, dst_ref=dst, send_sem=send_sem.at[sem], recv_sem=recv_sem.at[sem],
            device_id=device, device_id_type=MESH,
        )

    def feature(e):
        return (e // 4) * 4 + (e % 2) * 2 + (e // 2) % 2

    def columns(f):
        return pl.ds(pl.multiple_of(f * SHARE, 128), SHARE)

    def wide(i):
        return pl.ds(pl.multiple_of(i * WIDE, 128), WIDE)

    def chunk_rows(k):
        if isinstance(k, int):
            return pl.ds(k * CHUNK, CHUNK)
        return pl.ds(pl.multiple_of(k * CHUNK, CHUNK), CHUNK)

    loads = [
        pltpu.make_async_copy(w_down.at[0], W.at[own, 0], local_sem.at[0]),
        pltpu.make_async_copy(w_up.at[0], W.at[own, 1], local_sem.at[1]),
        pltpu.make_async_copy(stash, st, local_sem.at[2]),
        pltpu.make_async_copy(grad, gr, local_sem.at[3]),
        pltpu.make_async_copy(base, ba, local_sem.at[4]),
        pltpu.make_async_copy(gain, gain_in, local_sem.at[5]),
        pltpu.make_async_copy(mom_down.at[0], m1, local_sem.at[6]),
        pltpu.make_async_copy(mom_up.at[0], m2, local_sem.at[7]),
    ]
    for i in (0, 1, 5, 2, 3, 4, 6, 7):
        loads[i].start()

    barrier = pltpu.get_barrier_semaphore()
    partners = [(far, d), (z_down, d), (z_up, d), (s, d_pair), (s, d_core), (far, d_pair), (15 - s, d)]
    partners += [(s, t) for t in d_x]
    for t in partners:
        pl.semaphore_signal(barrier, inc=1, device_id=t, device_id_type=MESH)
    pl.semaphore_wait(barrier, len(partners))

    w_pair = remote(W.at[own], W.at[own], 0, (s, d_pair))
    right, left = d_x[0], d_x[2]
    kinds = (yl, 1 - yl)

    def slot_of(o, kind):
        return ((x + 4 - o) % 4) * 4 + c * 2 + kinds[kind]

    w_right = [remote(W.at[slot_of(0, i)], W.at[slot_of(0, i)], 1 + i, (s, right)) for i in range(2)]
    w_left = [remote(W.at[slot_of(0, i)], W.at[slot_of(0, i)], 3 + i, (s, left)) for i in range(2)]
    w_on_right = [remote(W.at[slot_of(1, i), 0], W.at[slot_of(1, i), 0], 44 + i, (s, right)) for i in range(2)]
    w_on_left = [remote(W.at[slot_of(3, i), 1], W.at[slot_of(3, i), 1], 46 + i, (s, left)) for i in range(2)]

    def group(xs):
        return WS.at[pl.ds(xs * 4 + c * 2, 2)]

    def core_copy(o, kind):
        slot = W.at[slot_of(o, kind)]
        return remote(slot, slot, CORE + 2 * o + kind, (s, d_core))

    x_from = [(x + 4 - o) % 4 for o in range(4)]
    w_core = [[core_copy(o, kind) for kind in range(2)] for o in range(4)]
    ws_far = remote(W.at[own, 0], WS.at[own], 11, (far, d))
    ws_cross = remote(W.at[own, 0], WS.at[own], 26, (far, d_pair))
    ws_x = [remote(group(x), group(x), 12 + i, (s, t)) for i, t in enumerate(d_x)]
    ws_core = [remote(group(x_from[o]), group(x_from[o]), 15 + o, (s, d_core)) for o in range(4)]
    gain_copy = remote(gain_in, gain_land, 19, (far, d_pair))
    delta_copy = remote(delta_own, delta_far, 20, (far, d))
    low_copy = remote(low_own, low_far, 21, (far, d))
    part_copy = remote(part_send, part_recv, 22, (s, d_core))
    sum_copy = [remote(sum_send.at[(x + o) % 4], sum_recv.at[o - 1], 22 + o, (s, d_x[o - 1])) for o in (1, 2, 3)]
    final_copy = remote(final_send, final_recv, 5, (far, d))
    pair_copy = remote(pair_send, pair_recv, 27, (s, d_pair))

    def stash_copy(k):
        return remote(stash.at[chunk_rows(k)], sv.at[chunk_rows(k)], 28 + k, (far, d))

    def relay_part(k, i):
        part = sv.at[chunk_rows(k), pl.ds(i * PART, PART)]
        return remote(part, part, 48 + k * PARTS + i, (far, d))

    def direct_copy(k):
        return remote(sv.at[chunk_rows(k)], gp.at[chunk_rows(k)], 28 + CHUNKS + k, (15 - s, d))

    def z_part(k, i):
        part = (chunk_rows(k), pl.ds(i * PART, PART))
        return remote(sv.at[part], gp.at[part], 28 + CHUNKS + k, (z_down, d))

    def z_copy(k):
        return remote(sv.at[chunk_rows(k)], gp.at[chunk_rows(k)], 28 + CHUNKS + k, (z_down, d))

    loads[0].wait()
    loads[1].wait()
    w_pair.start()
    w_right[0].start()
    w_left[0].start()
    ws_cross.start()
    ws_far.start()
    w_core[0][0].start()
    loads[5].wait()
    gain_copy.start()

    def pump(k):
        if k < 3:
            @pl.when(s != 8)
            def _():
                stash_copy(k).start()
        else:
            @pl.when(jnp.logical_and(s != 8, s != 0))
            def _():
                stash_copy(k).start()

    def pump_rest():
        @pl.when(s == 0)
        def _():
            for k in range(3, CHUNKS):
                stash_copy(k).start()

    pump(0)
    gain_own[...] = gain_in[...].astype(f32)

    loads[2].wait()

    def mean_and_inverse(ref, rows, extra=None):
        def add(i, acc):
            return acc + fold(ref[rows, wide(i)].astype(f32))

        zero = jnp.zeros((CHUNK, 128), f32)
        mean = row_sum(lax.fori_loop(0, WIDES, add, zero)) * (1.0 / D)

        def add_square(i, acc):
            centred = ref[rows, wide(i)].astype(f32) - mean
            total = acc[0] + fold(centred * centred)
            if extra is None:
                return (total,)
            return (total, acc[1] + fold(centred * extra[rows, wide(i)]))

        sums = lax.fori_loop(0, WIDES, add_square, (zero,) if extra is None else (zero, zero))
        inverse = lax.rsqrt(row_sum(sums[0]) * (1.0 / D) + norm_eps)
        if extra is None:
            return mean, inverse
        return mean, inverse, row_sum(sums[1]) * (1.0 / D)

    def row_stats(r, carry):
        rows = chunk_rows(r)
        mean, inverse = mean_and_inverse(st, rows)
        mean_row[rows, :] = mean
        inv_row[rows, :] = inverse
        return carry

    lax.fori_loop(0, CHUNKS, row_stats, 0)

    w_pair.wait_recv()
    w_right[1].start()
    w_left[1].start()
    w_core[0][1].start()
    pump(1)

    def pass_on(i):
        w_right[i].wait_recv()
        w_on_right[i].start()
        w_core[1][i].start()
        w_left[i].wait_recv()
        w_on_left[i].start()
        w_core[3][i].start()

    def end_group(i):
        w_on_right[i].wait_recv()
        w_on_left[i].wait_recv()
        w_core[2][i].start()

    def add_delta(o, acc):
        e = x_from[o] * 4
        for i in range(4):
            acc = acc + dot_last(gr[:, columns(feature(e + i))], W[e + i, 1])
        return acc

    def group_ready(o):
        w_core[o][0].wait_recv()
        w_core[o][1].wait_recv()

    def write_normed(r, carry):
        rows = chunk_rows(r)
        mean, inverse = mean_row[rows, :], inv_row[rows, :]

        def one(i, carry):
            centred = st[rows, wide(i)].astype(f32) - mean
            st[rows, wide(i)] = ((centred * inverse) * gain_far[:, wide(i)]).astype(bf16)
            return carry

        return lax.fori_loop(0, WIDES, one, carry)

    pass_on(0)
    loads[3].wait()
    group_ready(0)
    delta = add_delta(0, jnp.zeros((ROWS, RANK), f32))
    pass_on(1)
    gain_copy.wait_recv()
    gain_far[...] = gain_land[...].astype(f32)
    group_ready(1)
    delta = add_delta(1, delta)
    group_ready(3)
    delta = add_delta(3, delta)
    end_group(0)
    lax.fori_loop(0, 2, write_normed, 0)
    end_group(1)
    ws_far.wait_recv()
    ws_cross.wait_recv()
    for copy in ws_x:
        copy.start()
    ws_core[0].start()
    group_ready(2)
    delta = add_delta(2, delta)
    delta_own[...] = jnp.zeros((ROWS, 128), bf16)
    delta_own[:, :RANK] = delta.astype(bf16)
    delta_copy.start()
    pump(2)

    def fill_b(start, count):
        rows = pl.ds(start, count)

        def write_b(g, acc):
            for i in range(4):
                e = g * 4 + i
                cols = columns(feature(e))
                back = jnp.dot(delta_own[rows, :RANK], W[e, 0], preferred_element_type=f32)
                value = (ba[rows, cols].astype(f32) + back) * gain_own[:, cols]
                b[rows, cols] = value
                acc = acc + fold(value)
            return acc

        b_sum = lax.fori_loop(0, 4, write_b, jnp.zeros((count, 128), f32))
        b_mean[rows, :] = row_sum(b_sum) * (1.0 / D)

    loads[4].wait()
    fill_b(0, 2 * CHUNK)

    def grad_chunk(k):
        rows = chunk_rows(k)
        mean, inverse, cross = mean_and_inverse(sv, rows, b)
        first_mean = b_mean[rows, :]
        second_mean = cross * inverse

        def one(i, carry):
            unit = (sv[rows, wide(i)].astype(f32) - mean) * inverse
            value = inverse * (b[rows, wide(i)] - first_mean - unit * second_mean)
            sv[rows, wide(i)] = value.astype(bf16)
            return carry

        lax.fori_loop(0, WIDES, one, 0)

    def step(k):
        @pl.when(s != 0)
        def _():
            stash_copy(k).wait_recv()
            grad_chunk(k)

        @pl.when(s == 8)
        def _():
            if k == CHUNKS - 1:
                direct_copy(k).start()
            else:
                for i in range(PARTS):
                    relay_part(k, i).start()

        @pl.when(jnp.logical_and(s != 0, s != 8))
        def _():
            z_copy(k).start()

        if k > 0:
            relay(k - 1)

    def relay(k):
        @pl.when(s == 0)
        def _():
            for i in range(PARTS):
                relay_part(k, i).wait_recv()
                z_part(k, i).start()

    step(0)
    fill_b(2 * CHUNK, ROWS - 2 * CHUNK)
    lax.fori_loop(2, CHUNKS, write_normed, 0)
    step(1)

    for o in (1, 3, 2):
        ws_x[o - 1].wait_recv()
        ws_core[o].start()
    for o in (0, 1, 3, 2):
        ws_core[o].wait_recv()

    def add_low(g, acc):
        for i in range(4):
            e = g * 4 + i
            acc = acc + dot_last(st[:, columns(feature(e))], WS[e])
        return acc

    low = lax.fori_loop(0, 4, add_low, jnp.zeros((ROWS, RANK), f32))
    low_own[...] = jnp.zeros((ROWS, 128), bf16)
    low_own[:, :RANK] = low.astype(bf16)
    low_copy.start()
    pump(3)
    pump_rest()
    step(2)
    pump(4)

    delta_copy.wait_recv()
    low_copy.wait_recv()
    delta_t = delta_far[...].astype(f32).T[:RANK].astype(bf16)
    low_t = low_far[...].astype(f32).T[:RANK].astype(bf16)

    def write_parts(j, carry):
        f = (j // 2) * 4 + (j % 2) * 2
        for buf, core in ((part_keep, c), (part_send, 1 - c)):
            cols = columns(f + core)
            one = jnp.dot(delta_t, st[:, cols], preferred_element_type=f32) * (1.0 / TOKENS)
            two = jnp.dot(low_t, gr[:, cols], preferred_element_type=f32) * (1.0 / TOKENS)
            buf[j, 0] = one.astype(bf16)
            buf[j, 1] = two.astype(bf16)
        return carry

    lax.fori_loop(0, 8, write_parts, 0)
    part_copy.start()
    step(3)
    pump(5)

    part_copy.wait_recv()

    def add_parts(j, carry):
        total = part_keep[j].astype(f32) + part_recv[j].astype(f32)
        sum_send[j // 2, j % 2] = total.astype(bf16)
        return carry

    lax.fori_loop(0, 8, add_parts, 0)
    for copy in sum_copy:
        copy.start()

    step(4)
    pump(6)
    step(5)
    pump(7)

    for copy in sum_copy:
        copy.wait_recv()

    def total_of(y, kind):
        total = sum_send[x, y, kind].astype(f32)
        for i in range(3):
            total = total + sum_recv[i, y, kind].astype(f32)
        return total

    for kind in range(2):
        pair_send[kind] = total_of(1 - yl, kind).astype(bf16)
        kept[kind] = total_of(yl, kind)
    pair_copy.start()

    step(6)
    step(7)

    pair_copy.wait_recv()
    final_send[...] = (kept[0] + pair_recv[0].astype(f32)).astype(bf16)
    final_copy.start()
    loads[7].wait()
    step2[...], new2[...] = lion(m2[...].astype(f32), kept[1] + pair_recv[1].astype(f32))
    final_copy.wait_recv()
    loads[6].wait()
    step1[...], new1[...] = lion(m1[...].astype(f32), final_recv[...].astype(f32))

    @pl.when(s == 15)
    def _():
        ba[...] = jnp.zeros_like(ba)
        zeros = pltpu.make_async_copy(ba, gp, local_sem.at[8])
        zeros.start()
        zeros.wait()

    sent = [w_pair, *w_right, *w_left, *w_on_right, *w_on_left, ws_far, ws_cross, *ws_x, *ws_core]
    sent += [copy for pair_of in w_core for copy in pair_of]
    sent += [gain_copy, delta_copy, low_copy, part_copy, *sum_copy, pair_copy, final_copy]
    for copy in sent:
        copy.wait_send()
    for k in range(CHUNKS):
        @pl.when(s != 8)
        def _():
            stash_copy(k).wait_send()
            if k < CHUNKS - 1:
                z_copy(k).wait_send()

        @pl.when(s == 8)
        def _():
            if k < CHUNKS - 1:
                for i in range(PARTS):
                    relay_part(k, i).wait_send()

        if k == CHUNKS - 1:
            @pl.when(s != 0)
            def _():
                z_copy(k).wait_send()

        @pl.when(s != 15)
        def _():
            z_copy(k).wait_recv()


def finish_kernel(rows, a, b, c, d, rows_out, a_out, b_out, c_out, d_out, held, small, sem_in, sem_out):
    moves = [(a, small.at[0], a_out), (b, small.at[1], b_out), (c, small.at[2], c_out), (d, small.at[3], d_out)]
    for k in range(CHUNKS):
        part = pl.ds(k * CHUNK, CHUNK)
        moves.append((rows.at[part], held.at[part], rows_out.at[part]))
    into = [pltpu.make_async_copy(m[0], m[1], sem_in.at[i]) for i, m in enumerate(moves)]
    out = [pltpu.make_async_copy(m[1], m[2], sem_out.at[i]) for i, m in enumerate(moves)]
    for copy in into:
        copy.start()
    for first, second in zip(into, out):
        first.wait()
        second.start()
    for copy in out:
        copy.wait()


def shards(stash, grad_in, base_back, gain, w_down, w_up, mom_down, mom_up):
    hbm = pl.BlockSpec(memory_space=pltpu.HBM)
    vmem = pl.BlockSpec(memory_space=pltpu.VMEM)
    share = (RANK, SHARE)
    maps = jax.ShapeDtypeStruct(share, bf16)
    shapes = (jax.ShapeDtypeStruct((ROWS, D), bf16), maps, maps, maps, maps)
    outs = pl.pallas_call(
        main_kernel,
        out_shape=shapes,
        in_specs=[hbm] * 8,
        out_specs=(hbm, vmem, vmem, vmem, vmem),
        scratch_shapes=[
            pltpu.VMEM(share, bf16),
            pltpu.VMEM(share, bf16),
            pltpu.VMEM((1, D), bf16),
            pltpu.VMEM((1, D), bf16),
            pltpu.VMEM((ROWS, D), bf16),
            pltpu.VMEM((ROWS, D), bf16),
            pltpu.VMEM((ROWS, D), bf16),
            pltpu.VMEM((ROWS, D), bf16),
            pltpu.VMEM((ROWS, D), f32),
            pltpu.VMEM((16, 2) + share, bf16),
            pltpu.VMEM((16,) + share, bf16),
            pltpu.VMEM((1, D), f32),
            pltpu.VMEM((1, D), f32),
            pltpu.VMEM((ROWS, 128), bf16),
            pltpu.VMEM((ROWS, 128), bf16),
            pltpu.VMEM((ROWS, 128), bf16),
            pltpu.VMEM((ROWS, 128), bf16),
            pltpu.VMEM((ROWS, 1), f32),
            pltpu.VMEM((ROWS, 1), f32),
            pltpu.VMEM((ROWS, 1), f32),
            pltpu.VMEM((8, 2) + share, bf16),
            pltpu.VMEM((8, 2) + share, bf16),
            pltpu.VMEM((8, 2) + share, bf16),
            pltpu.VMEM((4, 2, 2) + share, bf16),
            pltpu.VMEM((3, 2, 2) + share, bf16),
            pltpu.VMEM((2,) + share, bf16),
            pltpu.VMEM((2,) + share, bf16),
            pltpu.VMEM((2,) + share, f32),
            pltpu.VMEM(share, bf16),
            pltpu.VMEM(share, bf16),
            pltpu.SemaphoreType.DMA((9,)),
            pltpu.SemaphoreType.DMA((SEMS,)),
            pltpu.SemaphoreType.DMA((SEMS,)),
        ],
        compiler_params=pltpu.CompilerParams(
            collective_id=0, has_side_effects=True, vmem_limit_bytes=VMEM_LIMIT
        ),
        cost_estimate=pl.CostEstimate(flops=2 * 5 * ROWS * D * RANK, bytes_accessed=16 * ROWS * D, transcendentals=0),
        name="block",
    )(stash[0], grad_in[0], base_back[0], gain, w_down, w_up, mom_down, mom_up)
    outs = pl.pallas_call(
        finish_kernel,
        out_shape=shapes,
        in_specs=[hbm] * 5,
        out_specs=(hbm,) * 5,
        scratch_shapes=[
            pltpu.VMEM((ROWS, D), bf16),
            pltpu.VMEM((4,) + share, bf16),
            pltpu.SemaphoreType.DMA((CHUNKS + 4,)),
            pltpu.SemaphoreType.DMA((CHUNKS + 4,)),
        ],
        compiler_params=pltpu.CompilerParams(vmem_limit_bytes=VMEM_LIMIT),
        name="finish",
    )(*outs)
    return tuple(out[None] for out in outs)


def solution(mesh):
    rows = P("pipe", "dp", None)
    share = P("pipe", None, "dp")
    return jax.shard_map(
        shards,
        mesh=mesh,
        in_specs=(rows, rows, rows, P("pipe", None), share, share, share, share),
        out_specs=(rows, share, share, share, share),
        check_vma=False,
    )
```

```python
import functools

import jax
import jax.numpy as jnp
from jax import lax
from jax.experimental import pallas as pl
from jax.experimental.pallas import tpu as pltpu
from jax.sharding import PartitionSpec as P

norm_eps = 1e-05
beta_one = 0.9
beta_two = 0.99
lion_delta = 0.003

D = 12288
RANK = 64
ROWS = 128
TOKENS = 2048
SHARE = D // 16
CHUNK = 16
CHUNKS = ROWS // CHUNK
WIDE = 1536
WIDES = D // WIDE
CORE = 48
HALF = CORE + 8
SEMS = HALF + 11
MESH = pl.DeviceIdType.MESH
VMEM_LIMIT = 63 * 1024 * 1024
f32 = jnp.float32
bf16 = jnp.bfloat16

contract_last = (((1,), (1,)), ((), ()))


def dot_last(a, b):
    return lax.dot_general(a, b, contract_last, preferred_element_type=f32)


def fold(v):
    parts = [v[:, i : i + 128] for i in range(0, v.shape[1], 128)]
    while len(parts) > 1:
        half = [a + b for a, b in zip(parts[::2], parts[1::2])]
        if len(parts) % 2:
            half.append(parts[-1])
        parts = half
    return parts[0]


def row_sum(acc):
    return jnp.sum(acc, axis=1, keepdims=True)


def lion(moment, gradient):
    blend = beta_one * moment + (1.0 - beta_one) * gradient
    direction = (blend / (jnp.abs(blend) + lion_delta)).astype(bf16)
    renewed = (beta_two * moment + (1.0 - beta_two) * gradient).astype(bf16)
    return direction, renewed


def main_kernel(
    stash, grad, base, gain, w_down, w_up, mom_down, mom_up,
    gp, step1, step2, new1, new2,
    results,    m1, m2,    gain_in, gain_land, st, sv, gr, ba, b, W, WS, gain_own, gain_far,
    delta_sum, delta_own, delta_far, low_own, low_far, b_mean, mean_row, inv_row,
    part_send, part_keep, part_recv, sum_send, sum_recv,
    total_send, total_recv, kept,
    local_sem, send_sem, recv_sem,
):
    s = lax.axis_index("pipe")
    d = lax.axis_index("dp")
    x, yl, c = d // 4, (d // 2) % 2, d % 2
    far = (s + 8) % 16
    with_down = jnp.logical_and(s != 0, s != 8)
    z = s % 8
    z_down = s - z + (z + 7) % 8
    z_up = s - z + (z + 1) % 8
    d_pair = d + 2 - 4 * yl
    d_core = d + 1 - 2 * c
    d_x = [(d + 4 * o) % 16 for o in (1, 2, 3)]
    own = x * 4 + c * 2 + yl
    pair = x * 4 + c * 2 + 1 - yl
    first = x * 4 + c * 2

    def remote(src, dst, sem, device):
        return pltpu.make_async_remote_copy(
            src_ref=src, dst_ref=dst, send_sem=send_sem.at[sem], recv_sem=recv_sem.at[sem],
            device_id=device, device_id_type=MESH,
        )

    def feature(e):
        return (e // 4) * 4 + (e % 2) * 2 + (e // 2) % 2

    def columns(f):
        return pl.ds(pl.multiple_of(f * SHARE, 128), SHARE)

    def wide(i):
        return pl.ds(pl.multiple_of(i * WIDE, 128), WIDE)

    def chunk_rows(k):
        if isinstance(k, int):
            return pl.ds(k * CHUNK, CHUNK)
        return pl.ds(pl.multiple_of(k * CHUNK, CHUNK), CHUNK)

    loads = [
        pltpu.make_async_copy(w_down.at[0], W.at[own, 0], local_sem.at[0]),
        pltpu.make_async_copy(w_up.at[0], W.at[own, 1], local_sem.at[1]),
        pltpu.make_async_copy(gain, gain_in, local_sem.at[5]),
        pltpu.make_async_copy(stash, st, local_sem.at[2]),
        pltpu.make_async_copy(grad, gr, local_sem.at[3]),
        pltpu.make_async_copy(mom_down.at[0], m1, local_sem.at[6]),
        pltpu.make_async_copy(mom_up.at[0], m2, local_sem.at[7]),
    ]
    for load in loads:
        load.start()

    base_load = pltpu.make_async_copy(base, ba, local_sem.at[4])
    saved_load = pltpu.make_async_copy(stash, sv, local_sem.at[4])
    pl.when(s != 0)(base_load.start)
    pl.when(s == 0)(saved_load.start)

    barrier = pltpu.get_barrier_semaphore()
    partners = [(far, d), (z_down, d), (z_up, d), (s, d_pair), (s, d_core), (far, d_pair)]
    partners += [(s, t) for t in d_x]
    for t in partners:
        pl.semaphore_signal(barrier, inc=1, device_id=t, device_id_type=MESH)
    pl.semaphore_wait(barrier, len(partners))

    w_pair = [remote(W.at[own, j], W.at[own, j], (0, HALF + 8)[j], (s, d_pair)) for j in range(2)]
    right, left = d_x[0], d_x[2]
    kinds = (yl, 1 - yl)

    def slot_of(o, kind):
        return ((x + 4 - o) % 4) * 4 + c * 2 + kinds[kind]

    def half_to(i, j, sem, t):
        half = W.at[slot_of(0, i), j]
        return remote(half, half, HALF + sem + 2 * i + j, (s, t))

    w_right = [[half_to(i, j, 0, right) for j in range(2)] for i in range(2)]
    w_left = [[half_to(i, j, 4, left) for j in range(2)] for i in range(2)]
    w_on_right = [remote(W.at[slot_of(1, i), 0], W.at[slot_of(1, i), 0], 44 + i, (s, right)) for i in range(2)]
    w_on_left = [remote(W.at[slot_of(3, i), 1], W.at[slot_of(3, i), 1], 46 + i, (s, left)) for i in range(2)]

    def group(xs):
        return WS.at[pl.ds(xs * 4 + c * 2, 2)]

    def core_copy(o, kind):
        slot = W.at[slot_of(o, kind)]
        return remote(slot, slot, CORE + 2 * o + kind, (s, d_core))

    x_from = [(x + 4 - o) % 4 for o in range(4)]
    w_core = [[core_copy(o, kind) for kind in range(2)] for o in range(4)]
    ws_far = remote(W.at[own, 0], WS.at[own], 11, (far, d))
    ws_cross = remote(W.at[own, 0], WS.at[own], 26, (far, d_pair))
    ws_x = [remote(group(x), group(x), 12 + i, (s, t)) for i, t in enumerate(d_x)]
    ws_core = [remote(group(x_from[o]), group(x_from[o]), 15 + o, (s, d_core)) for o in range(4)]
    gain_copy = remote(gain_in, gain_land, 19, (far, d_pair))
    delta_copy = remote(delta_own, delta_far, 20, (far, d))
    low_copy = remote(low_own, low_far, 21, (far, d))
    part_copy = remote(part_send, part_recv, 22, (s, d_core))
    sum_copy = [remote(sum_send.at[(x + o) % 4], sum_recv.at[o - 1], 22 + o, (s, d_x[o - 1])) for o in (1, 2, 3)]
    total_to = [(far, d), (far, d_pair), (s, d_pair)]
    total_copy = [remote(total_send.at[i], total_recv.at[i], (5, 6, 27)[i], to) for i, to in enumerate(total_to)]

    def stash_copy(k):
        return remote(stash.at[chunk_rows(k)], sv.at[chunk_rows(k)], 28 + k, (far, d))

    def base_copy(k):
        return remote(base.at[chunk_rows(k)], ba.at[chunk_rows(k)], 28 + k, (far, d))

    def base_half(j):
        half = (chunk_rows(1), pl.ds(j * (D // 2), D // 2))
        return remote(base.at[half], ba.at[half], HALF + 9 + j, (far, d))

    def z_copy(k):
        return remote(sv.at[chunk_rows(k)], gp.at[chunk_rows(k)], 28 + CHUNKS + k, (z_down, d))

    loads[0].wait()
    loads[1].wait()
    pl.when(s == 8)(ws_far.start)
    w_pair[0].start()
    w_pair[1].start()
    pl.when(with_down)(w_right[0][0].start)
    w_left[0][1].start()
    w_right[0][1].start()
    pl.when(with_down)(w_left[0][0].start)
    pl.when(s != 8)(ws_far.start)
    w_core[0][0].start()
    loads[2].wait()
    gain_copy.start()
    ws_cross.start()

    def pump(k):
        @pl.when(jnp.logical_and(s != 0, s != 8))
        def _():
            stash_copy(k).start()

        pl.when(s == 8)(base_half(0).start if k == 1 else base_copy(k).start)

    pump(0)
    gain_own[...] = gain_in[...].astype(f32)

    loads[3].wait()

    def mean_and_inverse(ref, rows, extra=None):
        def add(i, acc):
            return acc + fold(ref[rows, wide(i)].astype(f32))

        zero = jnp.zeros((CHUNK, 128), f32)
        mean = row_sum(lax.fori_loop(0, WIDES, add, zero)) * (1.0 / D)

        def add_square(i, acc):
            centred = ref[rows, wide(i)].astype(f32) - mean
            total = acc[0] + fold(centred * centred)
            if extra is None:
                return (total,)
            return (total, acc[1] + fold(centred * extra[rows, wide(i)]))

        sums = lax.fori_loop(0, WIDES, add_square, (zero,) if extra is None else (zero, zero))
        inverse = lax.rsqrt(row_sum(sums[0]) * (1.0 / D) + norm_eps)
        if extra is None:
            return mean, inverse
        return mean, inverse, row_sum(sums[1]) * (1.0 / D)

    def row_stats(r, carry):
        rows = chunk_rows(r)
        mean, inverse = mean_and_inverse(st, rows)
        mean_row[rows, :] = mean
        inv_row[rows, :] = inverse
        return carry

    lax.fori_loop(0, CHUNKS, row_stats, 0)

    def pass_on(i):
        @pl.when(with_down)
        def _():
            w_right[i][0].wait_recv()
            w_on_right[i].start()

        w_left[i][1].wait_recv()
        w_on_left[i].start()
        w_right[i][1].wait_recv()
        w_core[1][i].start()
        pl.when(with_down)(w_left[i][0].wait_recv)
        w_core[3][i].start()

    def end_group(i):
        pl.when(with_down)(w_on_right[i].wait_recv)
        w_on_left[i].wait_recv()
        w_core[2][i].start()

    def add_delta(o, acc):
        e = x_from[o] * 4
        for i in range(4):
            acc = acc + dot_last(gr[:, columns(feature(e + i))], W[e + i, 1])
        return acc

    def group_ready(o):
        w_core[o][0].wait_recv()
        w_core[o][1].wait_recv()

    def write_normed(r, carry):
        rows = chunk_rows(r)
        mean, inverse = mean_row[rows, :], inv_row[rows, :]

        def one(i, carry):
            centred = st[rows, wide(i)].astype(f32) - mean
            st[rows, wide(i)] = ((centred * inverse) * gain_far[:, wide(i)]).astype(bf16)
            return carry

        return lax.fori_loop(0, WIDES, one, carry)

    def pair_arrived():
        w_pair[0].wait_recv()
        pl.when(with_down)(w_right[1][0].start)
        w_pair[1].wait_recv()
        w_left[1][1].start()
        w_right[1][1].start()
        pl.when(with_down)(w_left[1][0].start)
        w_core[0][1].start()

    pl.when(c == 1)(pair_arrived)
    pass_on(0)
    pl.when(c == 0)(pair_arrived)
    pump(1)

    def ws_spread():
        ws_far.wait_recv()
        ws_cross.wait_recv()
        for copy in ws_x:
            copy.start()
        ws_core[0].start()

    def ws_pass_on():
        for o in (1, 3, 2):
            ws_x[o - 1].wait_recv()
            ws_core[o].start()

    def ws_ready():
        for o in (0, 1, 3, 2):
            ws_core[o].wait_recv()

    def gain_ready():
        gain_copy.wait_recv()
        gain_far[...] = gain_land[...].astype(f32)

    pl.when(s == 0)(ws_spread)
    loads[4].wait()
    group_ready(0)
    delta = add_delta(0, jnp.zeros((ROWS, RANK), f32))
    pass_on(1)
    group_ready(1)
    delta = add_delta(1, delta)
    end_group(0)
    group_ready(3)
    delta_sum[...] = add_delta(3, delta)

    def finish_delta():
        end_group(1)
        group_ready(2)
        delta_own[...] = jnp.zeros((ROWS, 128), bf16)
        delta_own[:, :RANK] = add_delta(2, delta_sum[...]).astype(bf16)
        delta_copy.start()

    pl.when(s != 0)(finish_delta)
    pl.when(s == 8)(base_half(1).start)
    pump(2)

    def fill_b(start, count):
        rows = pl.ds(start, count)

        def write_b(g, acc):
            for i in range(4):
                e = g * 4 + i
                cols = columns(feature(e))
                back = jnp.dot(delta_own[rows, :RANK], W[e, 0], preferred_element_type=f32)
                value = (ba[rows, cols].astype(f32) + back) * gain_own[:, cols]
                b[rows, cols] = value
                acc = acc + fold(value)
            return acc

        b_sum = lax.fori_loop(0, 4, write_b, jnp.zeros((count, 128), f32))
        b_mean[rows, :] = row_sum(b_sum) * (1.0 / D)

    pl.when(s != 0)(base_load.wait)

    @pl.when(with_down)
    def _():
        fill_b(0, 2 * CHUNK)

    @pl.when(s == 0)
    def _():
        ws_pass_on()
        ws_ready()
        gain_ready()
        delta_copy.wait_recv()
        saved_load.wait()


    def grad_chunk(k):
        rows = chunk_rows(k)
        mean, inverse, cross = mean_and_inverse(sv, rows, b)
        first_mean = b_mean[rows, :]
        second_mean = cross * inverse

        def one(i, carry):
            unit = (sv[rows, wide(i)].astype(f32) - mean) * inverse
            value = inverse * (b[rows, wide(i)] - first_mean - unit * second_mean)
            sv[rows, wide(i)] = value.astype(bf16)
            return carry

        lax.fori_loop(0, WIDES, one, 0)

    def fill_far(k):
        rows = chunk_rows(k)

        def write_far(g, acc):
            for i in range(4):
                e = g * 4 + i
                cols = columns(feature(e))
                back = jnp.dot(delta_far[rows, :RANK], WS[e], preferred_element_type=f32)
                value = (ba[rows, cols].astype(f32) + back) * gain_far[:, cols]
                b[rows, cols] = value
                acc = acc + fold(value)
            return acc

        b_sum = lax.fori_loop(0, 4, write_far, jnp.zeros((CHUNK, 128), f32))
        b_mean[rows, :] = row_sum(b_sum) * (1.0 / D)

    def step(k):
        @pl.when(s == 0)
        def _():
            for copy in (base_half(0), base_half(1)) if k == 1 else (base_copy(k),):
                copy.wait_recv()
            fill_far(k)

        @pl.when(jnp.logical_and(s != 0, s != 8))
        def _():
            stash_copy(k).wait_recv()

        @pl.when(s != 8)
        def _():
            grad_chunk(k)
            z_copy(k).start()

    step(0)
    pl.when(s != 0)(ws_spread)

    @pl.when(with_down)
    def _():
        fill_b(2 * CHUNK, ROWS - 2 * CHUNK)

    step(1)
    pump(3)
    pl.when(s == 0)(finish_delta)
    pl.when(s != 0)(gain_ready)
    lax.fori_loop(0, CHUNKS, write_normed, 0)
    pl.when(s != 0)(ws_pass_on)
    step(2)
    pl.when(s != 0)(ws_ready)

    def add_low(g, acc):
        for i in range(4):
            e = g * 4 + i
            acc = acc + dot_last(st[:, columns(feature(e))], WS[e])
        return acc

    low = lax.fori_loop(0, 4, add_low, jnp.zeros((ROWS, RANK), f32))
    low_own[...] = jnp.zeros((ROWS, 128), bf16)
    low_own[:, :RANK] = low.astype(bf16)
    low_copy.start()
    pump(4)
    step(3)
    pump(5)
    pl.when(s != 0)(delta_copy.wait_recv)

    low_copy.wait_recv()
    delta_t = delta_far[...].astype(f32).T[:RANK].astype(bf16)
    low_t = low_far[...].astype(f32).T[:RANK].astype(bf16)

    def write_parts(j, carry):
        f = (j // 2) * 4 + (j % 2) * 2
        for buf, core in ((part_keep, c), (part_send, 1 - c)):
            cols = columns(f + core)
            one = jnp.dot(delta_t, st[:, cols], preferred_element_type=f32) * (1.0 / TOKENS)
            two = jnp.dot(low_t, gr[:, cols], preferred_element_type=f32) * (1.0 / TOKENS)
            buf[j, 0] = one.astype(bf16)
            buf[j, 1] = two.astype(bf16)
        return carry

    lax.fori_loop(0, 8, write_parts, 0)
    part_copy.start()

    step(4)
    pump(6)
    part_copy.wait_recv()

    def add_parts(j, carry):
        total = part_keep[j].astype(f32) + part_recv[j].astype(f32)
        sum_send[j // 2, j % 2] = total.astype(bf16)
        return carry

    lax.fori_loop(0, 8, add_parts, 0)
    for copy in sum_copy:
        copy.start()

    step(5)
    pump(7)
    step(6)

    for copy in sum_copy:
        copy.wait_recv()

    def total_of(y, kind):
        total = sum_send[x, y, kind].astype(f32)
        for i in range(3):
            total = total + sum_recv[i, y, kind].astype(f32)
        return total

    total_send[0] = total_of(yl, 0).astype(bf16)
    total_send[1] = total_of(1 - yl, 0).astype(bf16)
    total_send[2] = total_of(1 - yl, 1).astype(bf16)
    kept[...] = total_of(yl, 1)
    for copy in total_copy:
        copy.start()

    step(7)

    for copy in total_copy:
        copy.wait_recv()
    loads[5].wait()
    loads[6].wait()
    grad_first = total_recv[0].astype(f32) + total_recv[1].astype(f32)
    results[0], results[2] = lion(m1[...].astype(f32), grad_first)
    results[1], results[3] = lion(m2[...].astype(f32), kept[...] + total_recv[2].astype(f32))
    stores = [pltpu.make_async_copy(results.at[i], out, local_sem.at[9 + i]) for i, out in enumerate((step1, step2, new1, new2))]
    for store in stores:
        store.start()

    @pl.when(s == 15)
    def _():
        ba[...] = jnp.zeros_like(ba)
        zeros = pltpu.make_async_copy(ba, gp, local_sem.at[8])
        zeros.start()
        zeros.wait()

    for store in stores:
        store.wait()

    down_sent = [w_right[0][0], w_right[1][0], w_left[0][0], w_left[1][0], *w_on_right]
    sent = [*w_pair, w_right[0][1], w_right[1][1], w_left[0][1], w_left[1][1], *w_on_left, ws_far, ws_cross, *ws_x, *ws_core]
    sent += [copy for pair_of in w_core for copy in pair_of]
    sent += [gain_copy, delta_copy, low_copy, part_copy, *sum_copy, *total_copy]
    for copy in sent:
        copy.wait_send()

    @pl.when(with_down)
    def _():
        for copy in down_sent:
            copy.wait_send()

    for k in range(CHUNKS):
        @pl.when(s != 0 if k != 1 else with_down)
        def _():
            stash_copy(k).wait_send()

        if k == 1:
            @pl.when(s == 8)
            def _():
                base_half(0).wait_send()
                base_half(1).wait_send()

        @pl.when(s != 8)
        def _():
            z_copy(k).wait_send()

        @pl.when(s != 15)
        def _():
            z_copy(k).wait_recv()


def finish_kernel(rows, a, b, c, d, rows_out, a_out, b_out, c_out, d_out, held, small, sem_in, sem_out):
    moves = [(a, small.at[0], a_out), (b, small.at[1], b_out), (c, small.at[2], c_out), (d, small.at[3], d_out)]
    for k in range(CHUNKS):
        part = pl.ds(k * CHUNK, CHUNK)
        moves.append((rows.at[part], held.at[part], rows_out.at[part]))
    into = [pltpu.make_async_copy(m[0], m[1], sem_in.at[i]) for i, m in enumerate(moves)]
    out = [pltpu.make_async_copy(m[1], m[2], sem_out.at[i]) for i, m in enumerate(moves)]
    for copy in into:
        copy.start()
    for first, second in zip(into, out):
        first.wait()
        second.start()
    for copy in out:
        copy.wait()


def shards(stash, grad_in, base_back, gain, w_down, w_up, mom_down, mom_up):
    hbm = pl.BlockSpec(memory_space=pltpu.HBM)
    share = (RANK, SHARE)
    maps = jax.ShapeDtypeStruct(share, bf16)
    shapes = (jax.ShapeDtypeStruct((ROWS, D), bf16), maps, maps, maps, maps)
    outs = pl.pallas_call(
        main_kernel,
        out_shape=shapes,
        in_specs=[hbm] * 8,
        out_specs=(hbm,) * 5,
        scratch_shapes=[
            pltpu.VMEM((4,) + share, bf16),
            pltpu.VMEM(share, bf16),
            pltpu.VMEM(share, bf16),
            pltpu.VMEM((1, D), bf16),
            pltpu.VMEM((1, D), bf16),
            pltpu.VMEM((ROWS, D), bf16),
            pltpu.VMEM((ROWS, D), bf16),
            pltpu.VMEM((ROWS, D), bf16),
            pltpu.VMEM((ROWS, D), bf16),
            pltpu.VMEM((ROWS, D), f32),
            pltpu.VMEM((16, 2) + share, bf16),
            pltpu.VMEM((16,) + share, bf16),
            pltpu.VMEM((1, D), f32),
            pltpu.VMEM((1, D), f32),
            pltpu.VMEM((ROWS, RANK), f32),
            pltpu.VMEM((ROWS, 128), bf16),
            pltpu.VMEM((ROWS, 128), bf16),
            pltpu.VMEM((ROWS, 128), bf16),
            pltpu.VMEM((ROWS, 128), bf16),
            pltpu.VMEM((ROWS, 1), f32),
            pltpu.VMEM((ROWS, 1), f32),
            pltpu.VMEM((ROWS, 1), f32),
            pltpu.VMEM((8, 2) + share, bf16),
            pltpu.VMEM((8, 2) + share, bf16),
            pltpu.VMEM((8, 2) + share, bf16),
            pltpu.VMEM((4, 2, 2) + share, bf16),
            pltpu.VMEM((3, 2, 2) + share, bf16),
            pltpu.VMEM((3,) + share, bf16),
            pltpu.VMEM((3,) + share, bf16),
            pltpu.VMEM(share, f32),
            pltpu.SemaphoreType.DMA((13,)),
            pltpu.SemaphoreType.DMA((SEMS,)),
            pltpu.SemaphoreType.DMA((SEMS,)),
        ],
        compiler_params=pltpu.CompilerParams(
            collective_id=0, has_side_effects=True, vmem_limit_bytes=VMEM_LIMIT
        ),
        cost_estimate=pl.CostEstimate(flops=2 * 5 * ROWS * D * RANK, bytes_accessed=16 * ROWS * D, transcendentals=0),
        name="block",
    )(stash[0], grad_in[0], base_back[0], gain, w_down, w_up, mom_down, mom_up)
    outs = pl.pallas_call(
        finish_kernel,
        out_shape=shapes,
        in_specs=[hbm] * 5,
        out_specs=(hbm,) * 5,
        scratch_shapes=[
            pltpu.VMEM((ROWS, D), bf16),
            pltpu.VMEM((4,) + share, bf16),
            pltpu.SemaphoreType.DMA((CHUNKS + 4,)),
            pltpu.SemaphoreType.DMA((CHUNKS + 4,)),
        ],
        compiler_params=pltpu.CompilerParams(vmem_limit_bytes=VMEM_LIMIT),
        name="finish",
    )(*outs)
    return tuple(out[None] for out in outs)


def solution(mesh):
    rows = P("pipe", "dp", None)
    share = P("pipe", None, "dp")
    return jax.shard_map(
        shards,
        mesh=mesh,
        in_specs=(rows, rows, rows, P("pipe", None), share, share, share, share),
        out_specs=(rows, share, share, share, share),
        check_vma=False,
    )
```

```python
import functools

import jax
import jax.numpy as jnp
from jax import lax
from jax.experimental import pallas as pl
from jax.experimental.pallas import tpu as pltpu
from jax.sharding import PartitionSpec as P

norm_eps = 1e-05
beta_one = 0.9
beta_two = 0.99
lion_delta = 0.003

D = 12288
RANK = 64
ROWS = 128
TOKENS = 2048
SHARE = D // 16
CHUNK = 16
CHUNKS = ROWS // CHUNK
WIDE = 1536
WIDES = D // WIDE
CORE = 48
HALF = CORE + 8
SEMS = HALF + 11
MESH = pl.DeviceIdType.MESH
VMEM_LIMIT = 63 * 1024 * 1024
f32 = jnp.float32
bf16 = jnp.bfloat16

contract_last = (((1,), (1,)), ((), ()))


def dot_last(a, b):
    return lax.dot_general(a, b, contract_last, preferred_element_type=f32)


def fold(v):
    parts = [v[:, i : i + 128] for i in range(0, v.shape[1], 128)]
    while len(parts) > 1:
        half = [a + b for a, b in zip(parts[::2], parts[1::2])]
        if len(parts) % 2:
            half.append(parts[-1])
        parts = half
    return parts[0]


def row_sum(acc):
    return jnp.sum(acc, axis=1, keepdims=True)


def lion(moment, gradient):
    blend = beta_one * moment + (1.0 - beta_one) * gradient
    direction = (blend / (jnp.abs(blend) + lion_delta)).astype(bf16)
    renewed = (beta_two * moment + (1.0 - beta_two) * gradient).astype(bf16)
    return direction, renewed


class Either:
    def __init__(self, chosen, one, other):
        self.pairs = ((chosen, one), (jnp.logical_not(chosen), other))

    def start(self):
        for flag, copy in self.pairs:
            pl.when(flag)(copy.start)

    def wait_recv(self):
        for flag, copy in self.pairs:
            pl.when(flag)(copy.wait_recv)

    def wait_send(self):
        for flag, copy in self.pairs:
            pl.when(flag)(copy.wait_send)


def main_kernel(
    stash, grad, base, gain, w_down, w_up, mom_down, mom_up,
    gp, step1, step2, new1, new2,
    results,    m1, m2,    gain_in, gain_land, st, sv, gr, ba, b, W, WS, gain_own, gain_far,
    delta_sum, delta_own, delta_far, low_own, low_far, b_mean, mean_row, inv_row,
    part_send, part_keep, part_recv, sum_send, sum_recv,
    total_send, total_recv, kept,
    local_sem, send_sem, recv_sem,
):
    s = lax.axis_index("pipe")
    d = lax.axis_index("dp")
    x, yl, c = d // 4, (d // 2) % 2, d % 2
    far = (s + 8) % 16
    with_down = jnp.logical_and(s != 0, s != 8)
    z = s % 8
    z_down = s - z + (z + 7) % 8
    z_up = s - z + (z + 1) % 8
    d_pair = d + 2 - 4 * yl
    d_core = d + 1 - 2 * c
    d_x = [(d + 4 * o) % 16 for o in (1, 2, 3)]
    own = x * 4 + c * 2 + yl
    pair = x * 4 + c * 2 + 1 - yl
    first = x * 4 + c * 2

    def remote(src, dst, sem, device):
        return pltpu.make_async_remote_copy(
            src_ref=src, dst_ref=dst, send_sem=send_sem.at[sem], recv_sem=recv_sem.at[sem],
            device_id=device, device_id_type=MESH,
        )

    def feature(e):
        return (e // 4) * 4 + (e % 2) * 2 + (e // 2) % 2

    def columns(f):
        return pl.ds(pl.multiple_of(f * SHARE, 128), SHARE)

    def wide(i):
        return pl.ds(pl.multiple_of(i * WIDE, 128), WIDE)

    def chunk_rows(k):
        if isinstance(k, int):
            return pl.ds(k * CHUNK, CHUNK)
        return pl.ds(pl.multiple_of(k * CHUNK, CHUNK), CHUNK)

    loads = [
        pltpu.make_async_copy(w_down.at[0], W.at[own, 0], local_sem.at[0]),
        pltpu.make_async_copy(w_up.at[0], W.at[own, 1], local_sem.at[1]),
        pltpu.make_async_copy(gain, gain_in, local_sem.at[5]),
        pltpu.make_async_copy(stash, st, local_sem.at[2]),
        pltpu.make_async_copy(grad, gr, local_sem.at[3]),
        pltpu.make_async_copy(mom_down.at[0], m1, local_sem.at[6]),
        pltpu.make_async_copy(mom_up.at[0], m2, local_sem.at[7]),
    ]
    for load in loads:
        load.start()

    base_load = pltpu.make_async_copy(base, ba, local_sem.at[4])
    saved_load = pltpu.make_async_copy(stash, sv, local_sem.at[4])
    pl.when(s != 0)(base_load.start)
    pl.when(s == 0)(saved_load.start)

    barrier = pltpu.get_barrier_semaphore()
    partners = [(far, d), (z_down, d), (z_up, d), (s, d_pair), (s, d_core), (far, d_pair)]
    partners += [(s, t) for t in d_x]
    for t in partners:
        pl.semaphore_signal(barrier, inc=1, device_id=t, device_id_type=MESH)
    pl.semaphore_wait(barrier, len(partners))

    w_pair = [remote(W.at[own, j], W.at[own, j], (0, HALF + 8)[j], (s, d_pair)) for j in range(2)]
    right, left = d_x[0], d_x[2]
    kinds = (yl, 1 - yl)

    def slot_of(o, kind):
        return ((x + 4 - o) % 4) * 4 + c * 2 + kinds[kind]

    def half_to(i, j, sem, t):
        half = W.at[slot_of(0, i), j]
        return remote(half, half, HALF + sem + 2 * i + j, (s, t))

    w_right = [[half_to(i, j, 0, right) for j in range(2)] for i in range(2)]
    w_left = [[half_to(i, j, 4, left) for j in range(2)] for i in range(2)]
    w_on_right = [remote(W.at[slot_of(1, i), 0], W.at[slot_of(1, i), 0], 44 + i, (s, right)) for i in range(2)]
    w_on_left = [remote(W.at[slot_of(3, i), 1], W.at[slot_of(3, i), 1], 46 + i, (s, left)) for i in range(2)]

    def group(xs):
        return WS.at[pl.ds(xs * 4 + c * 2, 2)]

    def core_copy(o, kind):
        slot, up = W.at[slot_of(o, kind)], W.at[slot_of(o, kind), 1]
        both = remote(slot, slot, CORE + 2 * o + kind, (s, d_core))
        return Either(with_down, both, remote(up, up, CORE + 2 * o + kind, (s, d_core)))

    x_from = [(x + 4 - o) % 4 for o in range(4)]
    w_core = [[core_copy(o, kind) for kind in range(2)] for o in range(4)]
    ws_far = remote(W.at[own, 0], WS.at[own], 11, (far, d))
    ws_cross = remote(W.at[own, 0], WS.at[own], 26, (far, d_pair))
    ws_x = [remote(group(x), group(x), 12 + i, (s, t)) for i, t in enumerate(d_x)]
    ws_core = [remote(group(x_from[o]), group(x_from[o]), 15 + o, (s, d_core)) for o in range(4)]
    gain_copy = remote(gain_in, gain_land, 19, (far, d_pair))
    delta_copy = remote(delta_own, delta_far, 20, (far, d))
    low_copy = remote(low_own, low_far, 21, (far, d))
    part_copy = remote(part_send, part_recv, 22, (s, d_core))
    sum_copy = [remote(sum_send.at[(x + o) % 4], sum_recv.at[o - 1], 22 + o, (s, d_x[o - 1])) for o in (1, 2, 3)]
    total_to = [(far, d), (far, d_pair), (s, d_pair)]
    total_copy = [remote(total_send.at[i], total_recv.at[i], (5, 6, 27)[i], to) for i, to in enumerate(total_to)]

    def stash_copy(k):
        return remote(stash.at[chunk_rows(k)], sv.at[chunk_rows(k)], 28 + k, (far, d))

    def base_copy(k):
        return remote(base.at[chunk_rows(k)], ba.at[chunk_rows(k)], 28 + k, (far, d))

    def base_half(j):
        half = (chunk_rows(1), pl.ds(j * (D // 2), D // 2))
        return remote(base.at[half], ba.at[half], HALF + 9 + j, (far, d))

    def z_copy(k):
        return remote(sv.at[chunk_rows(k)], gp.at[chunk_rows(k)], 28 + CHUNKS + k, (z_down, d))

    loads[0].wait()
    loads[1].wait()
    loads[2].wait()
    gain_copy.start()
    ws_cross.start()
    pl.when(with_down)(w_pair[0].start)
    w_pair[1].start()
    pl.when(jnp.logical_not(with_down))(w_pair[0].start)
    pl.when(with_down)(w_right[0][0].start)
    w_left[0][1].start()
    w_right[0][1].start()
    pl.when(with_down)(w_left[0][0].start)
    ws_far.start()
    w_core[0][0].start()

    def pump(k):
        @pl.when(jnp.logical_and(s != 0, s != 8))
        def _():
            stash_copy(k).start()

        pl.when(s == 8)(base_half(0).start if k == 1 else base_copy(k).start)

    pump(0)
    gain_own[...] = gain_in[...].astype(f32)

    loads[3].wait()

    def mean_and_inverse(ref, rows, extra=None):
        def add(i, acc):
            return acc + fold(ref[rows, wide(i)].astype(f32))

        zero = jnp.zeros((CHUNK, 128), f32)
        mean = row_sum(lax.fori_loop(0, WIDES, add, zero)) * (1.0 / D)

        def add_square(i, acc):
            centred = ref[rows, wide(i)].astype(f32) - mean
            total = acc[0] + fold(centred * centred)
            if extra is None:
                return (total,)
            return (total, acc[1] + fold(centred * extra[rows, wide(i)]))

        sums = lax.fori_loop(0, WIDES, add_square, (zero,) if extra is None else (zero, zero))
        inverse = lax.rsqrt(row_sum(sums[0]) * (1.0 / D) + norm_eps)
        if extra is None:
            return mean, inverse
        return mean, inverse, row_sum(sums[1]) * (1.0 / D)

    def row_stats(r, carry):
        rows = chunk_rows(r)
        mean, inverse = mean_and_inverse(st, rows)
        mean_row[rows, :] = mean
        inv_row[rows, :] = inverse
        return carry

    lax.fori_loop(0, CHUNKS, row_stats, 0)

    def pass_on(i):
        @pl.when(with_down)
        def _():
            w_right[i][0].wait_recv()
            w_on_right[i].start()

        w_left[i][1].wait_recv()
        w_on_left[i].start()
        w_right[i][1].wait_recv()
        w_core[1][i].start()
        pl.when(with_down)(w_left[i][0].wait_recv)
        w_core[3][i].start()

    def end_group(i):
        pl.when(with_down)(w_on_right[i].wait_recv)
        w_on_left[i].wait_recv()
        w_core[2][i].start()

    def add_delta(o, acc):
        e = x_from[o] * 4
        for i in range(4):
            acc = acc + dot_last(gr[:, columns(feature(e + i))], W[e + i, 1])
        return acc

    def group_ready(o):
        w_core[o][0].wait_recv()
        w_core[o][1].wait_recv()

    def write_normed(r, carry):
        rows = chunk_rows(r)
        mean, inverse = mean_row[rows, :], inv_row[rows, :]

        def one(i, carry):
            centred = st[rows, wide(i)].astype(f32) - mean
            st[rows, wide(i)] = ((centred * inverse) * gain_far[:, wide(i)]).astype(bf16)
            return carry

        return lax.fori_loop(0, WIDES, one, carry)

    def pair_arrived():
        pl.when(with_down)(w_pair[0].wait_recv)
        pl.when(with_down)(w_right[1][0].start)
        w_pair[1].wait_recv()
        w_left[1][1].start()
        w_right[1][1].start()
        pl.when(with_down)(w_left[1][0].start)
        w_core[0][1].start()

    pl.when(c == 1)(pair_arrived)
    pass_on(0)
    pl.when(c == 0)(pair_arrived)
    pump(1)

    def ws_spread():
        ws_far.wait_recv()
        ws_cross.wait_recv()
        for copy in ws_x:
            copy.start()
        ws_core[0].start()

    def ws_pass_on():
        for o in (1, 3, 2):
            ws_x[o - 1].wait_recv()
            ws_core[o].start()

    def ws_ready():
        for o in (0, 1, 3, 2):
            ws_core[o].wait_recv()

    def gain_ready():
        gain_copy.wait_recv()
        gain_far[...] = gain_land[...].astype(f32)

    pl.when(s == 0)(ws_spread)
    loads[4].wait()
    group_ready(0)
    delta = add_delta(0, jnp.zeros((ROWS, RANK), f32))
    pass_on(1)
    group_ready(1)
    delta = add_delta(1, delta)
    end_group(0)
    group_ready(3)
    delta_sum[...] = add_delta(3, delta)

    def finish_delta():
        end_group(1)
        group_ready(2)
        delta_own[...] = jnp.zeros((ROWS, 128), bf16)
        delta_own[:, :RANK] = add_delta(2, delta_sum[...]).astype(bf16)
        delta_copy.start()

    pl.when(s != 0)(finish_delta)
    pl.when(s == 8)(base_half(1).start)
    pump(2)

    def fill_b(start, count):
        rows = pl.ds(start, count)

        def write_b(g, acc):
            for i in range(4):
                e = g * 4 + i
                cols = columns(feature(e))
                back = jnp.dot(delta_own[rows, :RANK], W[e, 0], preferred_element_type=f32)
                value = (ba[rows, cols].astype(f32) + back) * gain_own[:, cols]
                b[rows, cols] = value
                acc = acc + fold(value)
            return acc

        b_sum = lax.fori_loop(0, 4, write_b, jnp.zeros((count, 128), f32))
        b_mean[rows, :] = row_sum(b_sum) * (1.0 / D)

    pl.when(s != 0)(base_load.wait)

    @pl.when(with_down)
    def _():
        fill_b(0, 2 * CHUNK)

    @pl.when(s == 0)
    def _():
        ws_pass_on()
        ws_ready()
        gain_ready()
        delta_copy.wait_recv()
        saved_load.wait()


    def grad_chunk(k):
        rows = chunk_rows(k)
        mean, inverse, cross = mean_and_inverse(sv, rows, b)
        first_mean = b_mean[rows, :]
        second_mean = cross * inverse

        def one(i, carry):
            unit = (sv[rows, wide(i)].astype(f32) - mean) * inverse
            value = inverse * (b[rows, wide(i)] - first_mean - unit * second_mean)
            sv[rows, wide(i)] = value.astype(bf16)
            return carry

        lax.fori_loop(0, WIDES, one, 0)

    def fill_far(k):
        rows = chunk_rows(k)

        def write_far(g, acc):
            for i in range(4):
                e = g * 4 + i
                cols = columns(feature(e))
                back = jnp.dot(delta_far[rows, :RANK], WS[e], preferred_element_type=f32)
                value = (ba[rows, cols].astype(f32) + back) * gain_far[:, cols]
                b[rows, cols] = value
                acc = acc + fold(value)
            return acc

        b_sum = lax.fori_loop(0, 4, write_far, jnp.zeros((CHUNK, 128), f32))
        b_mean[rows, :] = row_sum(b_sum) * (1.0 / D)

    def step(k):
        @pl.when(s == 0)
        def _():
            for copy in (base_half(0), base_half(1)) if k == 1 else (base_copy(k),):
                copy.wait_recv()
            fill_far(k)

        @pl.when(jnp.logical_and(s != 0, s != 8))
        def _():
            stash_copy(k).wait_recv()

        @pl.when(s != 8)
        def _():
            grad_chunk(k)
            z_copy(k).start()

    step(0)
    pl.when(s != 0)(ws_spread)

    @pl.when(with_down)
    def _():
        fill_b(2 * CHUNK, ROWS - 2 * CHUNK)

    step(1)
    pump(3)
    pl.when(s == 0)(finish_delta)
    pl.when(s != 0)(gain_ready)
    lax.fori_loop(0, CHUNKS, write_normed, 0)
    pl.when(s != 0)(ws_pass_on)
    step(2)
    pl.when(s != 0)(ws_ready)

    def add_low(g, acc):
        for i in range(4):
            e = g * 4 + i
            acc = acc + dot_last(st[:, columns(feature(e))], WS[e])
        return acc

    low = lax.fori_loop(0, 4, add_low, jnp.zeros((ROWS, RANK), f32))
    low_own[...] = jnp.zeros((ROWS, 128), bf16)
    low_own[:, :RANK] = low.astype(bf16)
    low_copy.start()
    pump(4)
    step(3)
    pump(5)
    pl.when(s != 0)(delta_copy.wait_recv)

    low_copy.wait_recv()
    delta_t = delta_far[...].astype(f32).T[:RANK].astype(bf16)
    low_t = low_far[...].astype(f32).T[:RANK].astype(bf16)

    def write_parts(j, carry):
        f = (j // 2) * 4 + (j % 2) * 2
        for buf, core in ((part_keep, c), (part_send, 1 - c)):
            cols = columns(f + core)
            one = jnp.dot(delta_t, st[:, cols], preferred_element_type=f32) * (1.0 / TOKENS)
            two = jnp.dot(low_t, gr[:, cols], preferred_element_type=f32) * (1.0 / TOKENS)
            buf[j, 0] = one.astype(bf16)
            buf[j, 1] = two.astype(bf16)
        return carry

    lax.fori_loop(0, 8, write_parts, 0)
    part_copy.start()

    step(4)
    pump(6)
    part_copy.wait_recv()

    def add_parts(j, carry):
        total = part_keep[j].astype(f32) + part_recv[j].astype(f32)
        sum_send[j // 2, j % 2] = total.astype(bf16)
        return carry

    lax.fori_loop(0, 8, add_parts, 0)
    for copy in sum_copy:
        copy.start()

    step(5)
    pump(7)
    step(6)

    for copy in sum_copy:
        copy.wait_recv()

    def total_of(y, kind):
        total = sum_send[x, y, kind].astype(f32)
        for i in range(3):
            total = total + sum_recv[i, y, kind].astype(f32)
        return total

    total_send[0] = total_of(yl, 0).astype(bf16)
    total_send[1] = total_of(1 - yl, 0).astype(bf16)
    total_send[2] = total_of(1 - yl, 1).astype(bf16)
    kept[...] = total_of(yl, 1)
    for copy in total_copy:
        copy.start()

    step(7)

    for copy in total_copy:
        copy.wait_recv()
    loads[5].wait()
    loads[6].wait()
    grad_first = total_recv[0].astype(f32) + total_recv[1].astype(f32)
    results[0], results[2] = lion(m1[...].astype(f32), grad_first)
    results[1], results[3] = lion(m2[...].astype(f32), kept[...] + total_recv[2].astype(f32))
    stores = [pltpu.make_async_copy(results.at[i], out, local_sem.at[9 + i]) for i, out in enumerate((step1, step2, new1, new2))]
    for store in stores:
        store.start()

    @pl.when(s == 15)
    def _():
        ba[...] = jnp.zeros_like(ba)
        zeros = pltpu.make_async_copy(ba, gp, local_sem.at[8])
        zeros.start()
        zeros.wait()

    for store in stores:
        store.wait()

    down_sent = [w_right[0][0], w_right[1][0], w_left[0][0], w_left[1][0], *w_on_right]
    sent = [*w_pair, w_right[0][1], w_right[1][1], w_left[0][1], w_left[1][1], *w_on_left, ws_far, ws_cross, *ws_x, *ws_core]
    sent += [copy for pair_of in w_core for copy in pair_of]
    sent += [gain_copy, delta_copy, low_copy, part_copy, *sum_copy, *total_copy]
    pl.when(jnp.logical_not(with_down))(w_pair[0].wait_recv)
    for copy in sent:
        copy.wait_send()

    @pl.when(with_down)
    def _():
        for copy in down_sent:
            copy.wait_send()

    for k in range(CHUNKS):
        @pl.when(s != 0 if k != 1 else with_down)
        def _():
            stash_copy(k).wait_send()

        if k == 1:
            @pl.when(s == 8)
            def _():
                base_half(0).wait_send()
                base_half(1).wait_send()

        @pl.when(s != 8)
        def _():
            z_copy(k).wait_send()

        @pl.when(s != 15)
        def _():
            z_copy(k).wait_recv()


def finish_kernel(rows, a, b, c, d, rows_out, a_out, b_out, c_out, d_out, held, small, sem_in, sem_out):
    moves = [(a, small.at[0], a_out), (b, small.at[1], b_out), (c, small.at[2], c_out), (d, small.at[3], d_out)]
    for k in range(CHUNKS):
        part = pl.ds(k * CHUNK, CHUNK)
        moves.append((rows.at[part], held.at[part], rows_out.at[part]))
    into = [pltpu.make_async_copy(m[0], m[1], sem_in.at[i]) for i, m in enumerate(moves)]
    out = [pltpu.make_async_copy(m[1], m[2], sem_out.at[i]) for i, m in enumerate(moves)]
    for copy in into:
        copy.start()
    for first, second in zip(into, out):
        first.wait()
        second.start()
    for copy in out:
        copy.wait()


def shards(stash, grad_in, base_back, gain, w_down, w_up, mom_down, mom_up):
    hbm = pl.BlockSpec(memory_space=pltpu.HBM)
    share = (RANK, SHARE)
    maps = jax.ShapeDtypeStruct(share, bf16)
    shapes = (jax.ShapeDtypeStruct((ROWS, D), bf16), maps, maps, maps, maps)
    outs = pl.pallas_call(
        main_kernel,
        out_shape=shapes,
        in_specs=[hbm] * 8,
        out_specs=(hbm,) * 5,
        scratch_shapes=[
            pltpu.VMEM((4,) + share, bf16),
            pltpu.VMEM(share, bf16),
            pltpu.VMEM(share, bf16),
            pltpu.VMEM((1, D), bf16),
            pltpu.VMEM((1, D), bf16),
            pltpu.VMEM((ROWS, D), bf16),
            pltpu.VMEM((ROWS, D), bf16),
            pltpu.VMEM((ROWS, D), bf16),
            pltpu.VMEM((ROWS, D), bf16),
            pltpu.VMEM((ROWS, D), f32),
            pltpu.VMEM((16, 2) + share, bf16),
            pltpu.VMEM((16,) + share, bf16),
            pltpu.VMEM((1, D), f32),
            pltpu.VMEM((1, D), f32),
            pltpu.VMEM((ROWS, RANK), f32),
            pltpu.VMEM((ROWS, 128), bf16),
            pltpu.VMEM((ROWS, 128), bf16),
            pltpu.VMEM((ROWS, 128), bf16),
            pltpu.VMEM((ROWS, 128), bf16),
            pltpu.VMEM((ROWS, 1), f32),
            pltpu.VMEM((ROWS, 1), f32),
            pltpu.VMEM((ROWS, 1), f32),
            pltpu.VMEM((8, 2) + share, bf16),
            pltpu.VMEM((8, 2) + share, bf16),
            pltpu.VMEM((8, 2) + share, bf16),
            pltpu.VMEM((4, 2, 2) + share, bf16),
            pltpu.VMEM((3, 2, 2) + share, bf16),
            pltpu.VMEM((3,) + share, bf16),
            pltpu.VMEM((3,) + share, bf16),
            pltpu.VMEM(share, f32),
            pltpu.SemaphoreType.DMA((13,)),
            pltpu.SemaphoreType.DMA((SEMS,)),
            pltpu.SemaphoreType.DMA((SEMS,)),
        ],
        compiler_params=pltpu.CompilerParams(
            collective_id=0, has_side_effects=True, vmem_limit_bytes=VMEM_LIMIT
        ),
        cost_estimate=pl.CostEstimate(flops=2 * 5 * ROWS * D * RANK, bytes_accessed=16 * ROWS * D, transcendentals=0),
        name="block",
    )(stash[0], grad_in[0], base_back[0], gain, w_down, w_up, mom_down, mom_up)
    outs = pl.pallas_call(
        finish_kernel,
        out_shape=shapes,
        in_specs=[hbm] * 5,
        out_specs=(hbm,) * 5,
        scratch_shapes=[
            pltpu.VMEM((ROWS, D), bf16),
            pltpu.VMEM((4,) + share, bf16),
            pltpu.SemaphoreType.DMA((CHUNKS + 4,)),
            pltpu.SemaphoreType.DMA((CHUNKS + 4,)),
        ],
        compiler_params=pltpu.CompilerParams(vmem_limit_bytes=VMEM_LIMIT),
        name="finish",
    )(*outs)
    return tuple(out[None] for out in outs)


def solution(mesh):
    rows = P("pipe", "dp", None)
    share = P("pipe", None, "dp")
    return jax.shard_map(
        shards,
        mesh=mesh,
        in_specs=(rows, rows, rows, P("pipe", None), share, share, share, share),
        out_specs=(rows, share, share, share, share),
        check_vma=False,
    )
```
